256 devices in a mesh: loop: 64 (over z_hi, x, y), head: 4 (over z_lo, core).
Axes of the slice: x: 4, y: 4, z: 8 (z_hi: 4, z_lo: 2; z = z_hi * 2 + z_lo), core: 2. Of those that a mesh axis runs over, the one named last changes fastest.
Arguments:
- query_left: bfloat16 [64, 32, 8, 128], P('loop', 'head'), may hold values from -6 to 6
- query_right: bfloat16 [64, 8, 4096], P('loop', None, 'head'), may hold values from -6 to 6
- train_left: bfloat16 [128, 32, 8, 128], P('loop', 'head'), may hold values from -6 to 6
- train_right: bfloat16 [128, 8, 4096], P('loop', None, 'head'), may hold values from -6 to 6
- basis: bfloat16 [32, 128, 128], P('head'), may hold values from -0.5 to 0.5
- eigen: bfloat16 [32, 128, 4096], P(None, None, 'head'), may hold values from 0.25 to 4
- counts: int32 [128], P('loop'), may hold values from 128 to 4096
Outputs:
- scores: float32 [64, 128], P('head', 'loop')
The draws below stay inside these ranges and needn't reach their ends.
All inputs are finite; a program needn't handle non-finite values.
Results may differ from the reference program's by a relative error of at most 0.006.
Values may be sent and summed in bfloat16 or wider, within the bound.
No kernel may reach another device: no remote copies, remote signals or barrier semaphores. Data moves between devices by JAX's collectives and lax.ppermute only.
A program may use at most 128 MiB of HBM per device.

```python
import math
import jax
import jax.numpy as jnp
from jax import lax

HEAD_COUNT = 32
HEAD_DIM = 128
MODEL_DIM = 4096
GRAD_RANK = 8
QUERIES = 64
TRAIN_SEQS = 128


def plant(drawn, stream_key, low, top_value):
    dims = drawn.shape
    place = [jax.random.randint(jax.random.fold_in(stream_key, axis), (), 0, dims[axis]) for axis in range(len(dims))]
    drawn = drawn.at[tuple(place)].set(low)
    longest = dims.index(max(dims))
    place[longest] = (place[longest] + 1) % dims[longest]
    return drawn.at[tuple(place)].set(top_value)


def block_scale(rng, shape, split, smallest, top_value):
    loudness, own = 1.0, jax.random.fold_in(rng, 6)
    for dim, parts in split:
        steps = jnp.exp(jax.random.uniform(jax.random.fold_in(own, dim), (parts,), jnp.float32, smallest / len(split), top_value / len(split)))
        loudness = loudness * jnp.repeat(steps, shape[dim] // parts).reshape([-1 if axis == dim else 1 for axis in range(len(shape))])
    return loudness


def scatter_about(own_key, dims, width, most, pieces=(), dtype=jnp.bfloat16):
    loudness = block_scale(own_key, dims, pieces, -0.22, 0.18) if pieces else 1.0
    values = jax.random.normal(own_key, dims, jnp.float32) * width * loudness
    return jnp.minimum(jnp.maximum(values, -most), most).astype(dtype)


def setup_inputs(seed: int = 0) -> dict:
    key_list = jax.random.split(jax.random.key(seed), 8)
    query_left = scatter_about(key_list[0], (QUERIES, HEAD_COUNT, GRAD_RANK, HEAD_DIM), 1.0, 6.0, ((0, 64), (1, 4)))
    query_right = scatter_about(key_list[1], (QUERIES, GRAD_RANK, MODEL_DIM), 1.0, 6.0, ((0, 64), (2, 4)))
    train_left = scatter_about(key_list[2], (TRAIN_SEQS, HEAD_COUNT, GRAD_RANK, HEAD_DIM), 1.0, 6.0, ((0, 64), (1, 4)))
    train_right = scatter_about(key_list[3], (TRAIN_SEQS, GRAD_RANK, MODEL_DIM), 1.0, 6.0, ((0, 64), (2, 4)))
    basis = scatter_about(key_list[4], (HEAD_COUNT, HEAD_DIM, HEAD_DIM), HEAD_DIM ** -0.5, 0.5, ((0, 4),))
    eigen = jnp.clip(jnp.exp(math.log(4.0) - 2.7725887 * jax.random.uniform(key_list[5], (HEAD_COUNT, HEAD_DIM, MODEL_DIM), jnp.float32) ** block_scale(key_list[5], (HEAD_COUNT, HEAD_DIM, MODEL_DIM), ((2, 4),), -0.2, 0.2)), 0.25, 4.0).astype(jnp.bfloat16)
    counts = plant(jax.random.randint(key_list[6], (TRAIN_SEQS,), 128, 4097), jax.random.fold_in(key_list[6], 1), 128, 4096).astype(jnp.int32)
    return {"query_left": query_left, "query_right": query_right, "train_left": train_left, "train_right": train_right, "basis": basis, "eigen": eigen, "counts": counts}


DAMPING = 0.1

def rotated(left, basis):
    product = jnp.einsum('nhri,hij->nhrj', left.astype(jnp.float32), basis.astype(jnp.float32))
    return lax.optimization_barrier(product.astype(jnp.bfloat16))

def head_scores(query_rot, query_right, train_rot, train_right, eigen):
    qright = query_right.astype(jnp.float32)
    tright = train_right.astype(jnp.float32)

    def per_head(running, items):
        train_head, query_head, eigen_head = items
        dense = jnp.einsum('sri,srj->sij', train_head.astype(jnp.float32), tright)
        scaled = (dense / (eigen_head.astype(jnp.float32) + DAMPING)).astype(jnp.bfloat16)
        scaled = lax.optimization_barrier(scaled)
        product = jnp.einsum('sij,prj->prsi', scaled.astype(jnp.float32), qright)
        return (running + jnp.einsum('prsi,pri->ps', product, query_head.astype(jnp.float32)), None)
    start = jnp.zeros((query_rot.shape[0], train_rot.shape[0]), jnp.float32)
    items = (jnp.swapaxes(train_rot, 0, 1), jnp.swapaxes(query_rot, 0, 1), eigen)
    total, _ = lax.scan(per_head, start, items)
    return total

def reference(query_left, query_right, train_left, train_right, basis, eigen, counts):
    query_rot = rotated(query_left, basis)
    train_rot = rotated(train_left, basis)
    raw = head_scores(query_rot, query_right, train_rot, train_right, eigen)
    factor = 1.0 / (GRAD_RANK * math.sqrt(HEAD_COUNT * HEAD_DIM * MODEL_DIM))
    weights = counts.astype(jnp.float32) / 2048.0
    return raw * weights[None, :] * factor
```

```python
import math

import jax
import jax.numpy as jnp
from jax import lax
from jax.experimental import pallas as pl
from jax.experimental.pallas import tpu as pltpu
from jax.sharding import PartitionSpec as P

HEAD_COUNT = 32
HEAD_DIM = 128
MODEL_DIM = 4096
GRAD_RANK = 8
QUERIES = 64
DAMPING = 0.1
FACTOR = 1.0 / (GRAD_RANK * math.sqrt(HEAD_COUNT * HEAD_DIM * MODEL_DIM))

N = 4
HEADS = 8
SEQS = 8
FEATURES = 1024
COLUMNS = QUERIES * GRAD_RANK
BLOCK = COLUMNS // N


def axis_shift(axis, step):
    pairs = []
    for z in range(N):
        for x in range(N):
            for y in range(N):
                to = {"z": z, "x": x, "y": y}
                to[axis] = (to[axis] + step) % N
                pairs.append((z * 16 + x * 4 + y, to["z"] * 16 + to["x"] * 4 + to["y"]))
    return pairs


def swap_shift(step):
    pairs = []
    for z in range(N):
        for x in range(N):
            for y in range(N):
                for g in range(N):
                    source = (z * 16 + x * 4 + y) * N + g
                    target = (((z + step) % N) * 16 + x * 4 + g) * N + y
                    pairs.append((source, target))
    return pairs


def along(axis, value, step):
    return lax.ppermute(value, "loop", axis_shift(axis, step))


def swapped(value, step):
    return lax.ppermute(value, ("loop", "head"), swap_shift(step))


def across_heads(value, mask):
    return lax.ppermute(value, "head", [(i, i ^ mask) for i in range(N)])


def rotated(left, basis):
    product = jnp.einsum("nhri,hij->nhrj", left, basis, preferred_element_type=jnp.float32)
    return product.astype(jnp.bfloat16)


def score_kernel(place, *refs):
    tl = refs[0:4]
    tr = refs[4:8]
    ql = refs[8:12]
    qr = refs[12:16]
    eigen, out = refs[16:18]
    tl_all, tr_all, qr_all, ql_head, scaled, total = refs[18:]
    z, x, y, g = (place[i] for i in range(4))
    head = pl.program_id(0)

    @pl.when(head == 0)
    def _():
        total[...] = jnp.zeros_like(total)
        for m in range(N):
            tl_all[lax.rem(y - (g ^ m) + N, N)] = tl[m][...]
        for k in range(N):
            tr_all[16 * k : 16 * (k + 1), :] = tr[k][...].reshape(16, FEATURES)
            for j in range(FEATURES // 128):
                qr_all[BLOCK * k : BLOCK * (k + 1), 128 * j : 128 * (j + 1)] = qr[k][:, :, j].reshape(BLOCK, 128)

    for m in range(N):
        block = ql[m][:, :, head].reshape(BLOCK, HEAD_DIM).astype(jnp.float32)
        ql_head[lax.rem(y - (g ^ m) + N, N)] = block.T

    inverse = 1.0 / (eigen[0].astype(jnp.float32) + DAMPING)
    left = tl_all[:, :, head].reshape(SEQS * GRAD_RANK, HEAD_DIM)
    left = jnp.concatenate([left] * SEQS, axis=1)
    own = lax.broadcasted_iota(jnp.int32, left.shape, 0) // GRAD_RANK
    own = own == lax.broadcasted_iota(jnp.int32, left.shape, 1) // HEAD_DIM
    left = jnp.where(own, left, jnp.zeros_like(left))
    dense = lax.dot_general(left, tr_all[...], (((0,), (0,)), ((), ())), preferred_element_type=jnp.float32)
    dense = dense.reshape(SEQS, HEAD_DIM, FEATURES) * inverse[None]
    scaled[...] = dense.astype(jnp.bfloat16).reshape(SEQS * HEAD_DIM, FEATURES)

    product = lax.dot_general(
        scaled[...], qr_all[...], (((1,), (1,)), ((), ())), preferred_element_type=jnp.float32
    )
    for k in range(N):
        part = product[:, BLOCK * k : BLOCK * (k + 1)].reshape(SEQS, HEAD_DIM, BLOCK)
        total[:, BLOCK * k : BLOCK * (k + 1)] += jnp.sum(part * ql_head[k][None], axis=1)

    @pl.when(head == HEADS - 1)
    def _():
        column = lax.broadcasted_iota(jnp.int32, (COLUMNS, QUERIES), 0)
        target = lax.broadcasted_iota(jnp.int32, (COLUMNS, QUERIES), 1)
        yq = (y - column // BLOCK) & 3
        xq = (x - (column // 32) % N) & 3
        zq = (z - (column // 8) % N) & 3
        pick = ((g ^ zq) * 16 + xq * 4 + yq == target).astype(jnp.float32)
        picked = lax.dot_general(
            total[...], pick, (((1,), (0,)), ((), ())),
            preferred_element_type=jnp.float32, precision=lax.Precision.HIGHEST,
        )
        for m in range(N):
            out[m] = picked[:, 16 * m : 16 * (m + 1)]


def partial_scores(place, tl, tr, ql, qr, eigen):
    whole = lambda a: pl.BlockSpec(a.shape, lambda h, p: (0,) * a.ndim)
    operands = [*tl, *tr, *ql, *qr]
    return pl.pallas_call(
        score_kernel,
        out_shape=jax.ShapeDtypeStruct((N, SEQS, 16), jnp.float32),
        grid_spec=pltpu.PrefetchScalarGridSpec(
            num_scalar_prefetch=1,
            grid=(HEADS,),
            in_specs=[whole(a) for a in operands]
            + [pl.BlockSpec((1, HEAD_DIM, FEATURES), lambda h, p: (HEADS * p[2] + h, 0, 0))],
            out_specs=pl.BlockSpec((N, SEQS, 16), lambda h, p: (0, 0, 0)),
            scratch_shapes=[
                pltpu.VMEM((N, 2, HEADS, GRAD_RANK, HEAD_DIM), jnp.bfloat16),
                pltpu.VMEM((SEQS * GRAD_RANK, FEATURES), jnp.bfloat16),
                pltpu.VMEM((COLUMNS, FEATURES), jnp.bfloat16),
                pltpu.VMEM((N, HEAD_DIM, BLOCK), jnp.float32),
                pltpu.VMEM((SEQS * HEAD_DIM, FEATURES), jnp.bfloat16),
                pltpu.VMEM((SEQS, COLUMNS), jnp.float32),
            ],
        ),
        compiler_params=pltpu.CompilerParams(vmem_limit_bytes=48 * 2**20),
    )(place, *operands, eigen)


def on_device(query_left, query_right, train_left, train_right, basis, eigen, counts):
    loop, g = lax.axis_index("loop"), lax.axis_index("head")
    place = jnp.stack([loop // 16, loop // 4 % 4, loop % 4, g]).astype(jnp.int32)

    right = query_right.reshape(GRAD_RANK, 8, 128).transpose(1, 0, 2)[None]
    rights = [right] + [along("z", right, s) for s in range(1, N)]
    query_rot = rotated(query_left, basis)
    lefts = [swapped(query_rot, s) for s in range(N)]
    train_rot = rotated(train_left, basis)
    train_rot = swapped(train_rot, 0)
    tr = [train_right] + [along("y", train_right, k) for k in range(1, N)]

    both = jnp.concatenate([jnp.concatenate([a, b], 1) for a, b in zip(lefts, rights, strict=True)], 0)
    both = jnp.stack([both] + [along("x", both, s) for s in range(1, N)])

    left, right = both[:, :, :8], both[:, :, 8:]
    tl = [train_rot] + [across_heads(train_rot, m) for m in range(1, N)]
    ql = [left] + [across_heads(left, m) for m in range(1, N)]
    qr = [right] + [along("y", right, k) for k in range(1, N)]

    partial = partial_scores(place, tl, tr, ql, qr, eigen)

    summed = sum([across_heads(partial[m], m) for m in range(1, N)], partial[0])
    summed = sum([along("y", summed[2 * k : 2 * k + 2], -k) for k in range(1, N)], summed[:2])
    weights = counts.astype(jnp.float32) / 2048.0
    return (summed * weights[:, None] * FACTOR).T


def solution(mesh):
    placed = (
        P("loop", "head", None, None),
        P("loop", None, "head"),
        P("loop", "head", None, None),
        P("loop", None, "head"),
        P("head", None, None),
        P(None, None, "head"),
        P("loop"),
    )
    return jax.shard_map(
        on_device, mesh=mesh, in_specs=placed, out_specs=P("head", "loop"), check_vma=False
    )
```

```python
import math

import jax
import jax.numpy as jnp
from jax import lax
from jax.experimental import pallas as pl
from jax.experimental.pallas import tpu as pltpu
from jax.sharding import PartitionSpec as P

HEAD_COUNT = 32
HEAD_DIM = 128
MODEL_DIM = 4096
GRAD_RANK = 8
QUERIES = 64
DAMPING = 0.1
FACTOR = 1.0 / (GRAD_RANK * math.sqrt(HEAD_COUNT * HEAD_DIM * MODEL_DIM))

N = 4
HEADS = 8
SEQS = 8
FEATURES = 1024
COLUMNS = QUERIES * GRAD_RANK
BLOCK = COLUMNS // N


def axis_shift(axis, step):
    pairs = []
    for z in range(N):
        for x in range(N):
            for y in range(N):
                to = {"z": z, "x": x, "y": y}
                to[axis] = (to[axis] + step) % N
                pairs.append((z * 16 + x * 4 + y, to["z"] * 16 + to["x"] * 4 + to["y"]))
    return pairs


def swap_shift(step):
    pairs = []
    for z in range(N):
        for x in range(N):
            for y in range(N):
                for g in range(N):
                    source = (z * 16 + x * 4 + y) * N + g
                    target = (((z + step) % N) * 16 + x * 4 + g) * N + y
                    pairs.append((source, target))
    return pairs


def along(axis, value, step):
    return lax.ppermute(value, "loop", axis_shift(axis, step))


def swapped(value, step):
    return lax.ppermute(value, ("loop", "head"), swap_shift(step))


def across_heads(value, mask):
    return lax.ppermute(value, "head", [(i, i ^ mask) for i in range(N)])


VMEM = pl.BlockSpec(memory_space=pltpu.VMEM)
SMEM = pl.BlockSpec(memory_space=pltpu.SMEM)
TILES = FEATURES // 128


def rotate_kernel(query, right, train, basis, left_out, right_out):
    for h in range(HEADS):
        left = jnp.concatenate([query[0, h], train[0, h], train[1, h]], axis=0)
        left = jnp.dot(left, basis[h], preferred_element_type=jnp.float32).astype(jnp.bfloat16)
        for n in range(3):
            left_out[n, h] = left[8 * n : 8 * (n + 1)]
    for j in range(TILES):
        right_out[0, j] = right[0, :, 128 * j : 128 * (j + 1)]


def rotated(query_left, query_right, train_left, basis):
    return pl.pallas_call(
        rotate_kernel,
        out_shape=(
            jax.ShapeDtypeStruct((3, HEADS, GRAD_RANK, HEAD_DIM), jnp.bfloat16),
            jax.ShapeDtypeStruct((1, TILES, GRAD_RANK, 128), jnp.bfloat16),
        ),
    )(query_left, query_right, train_left, basis)


def score_kernel(place, *refs):
    lefts = refs[0:4]
    rights = refs[4:8]
    eigen, out, tl_all, tr_all, qr_all, ql_head, scaled, total, eigen_all, sems = refs[8:]
    z, x, y, g = (place[i] for i in range(4))
    fetches = [
        pltpu.make_async_copy(eigen.at[HEADS * y + h], eigen_all.at[h], sems.at[h]) for h in range(HEADS)
    ]
    for fetch in fetches:
        fetch.start()

    total[...] = jnp.zeros_like(total)
    for m in range(N):
        tl_all[lax.rem(y - (g ^ m) + N, N)] = lefts[m][16:]
    for k in range(N):
        m = g ^ ((y - k) & 3)
        columns = pl.ds(pl.multiple_of(m * BLOCK, BLOCK), BLOCK)
        for j in range(TILES):
            tile = slice(128 * j, 128 * (j + 1))
            tr_all[16 * k : 16 * (k + 1), tile] = rights[k][16:, j].reshape(16, 128)
            qr_all[tile, columns] = rights[k][:16, j].reshape(BLOCK, 128).T

    def expand(head, slot):
        pltpu.make_async_copy(eigen.at[HEADS * y + head], eigen_all.at[head], sems.at[head]).wait()
        inverse = 1.0 / (eigen_all[head].astype(jnp.float32) + DAMPING)
        left = tl_all[:, :, head].reshape(SEQS * GRAD_RANK, HEAD_DIM)
        left = jnp.concatenate([left] * SEQS, axis=1)
        own = lax.broadcasted_iota(jnp.int32, left.shape, 0) // GRAD_RANK
        own = own == lax.broadcasted_iota(jnp.int32, left.shape, 1) // HEAD_DIM
        left = jnp.where(own, left, jnp.zeros_like(left))
        dense = lax.dot_general(left, tr_all[...], (((0,), (0,)), ((), ())), preferred_element_type=jnp.float32)
        dense = dense.reshape(SEQS, HEAD_DIM, FEATURES) * inverse[None]
        scaled[slot] = dense.astype(jnp.bfloat16).reshape(SEQS * HEAD_DIM, FEATURES)

    def multiply(head, slot):
        for m in range(N):
            block = lefts[m][:16, head].reshape(BLOCK, HEAD_DIM)
            ql_head[:, BLOCK * m : BLOCK * (m + 1)] = block.astype(jnp.float32).T
        product = jnp.dot(scaled[slot], qr_all[...], preferred_element_type=jnp.float32)
        product = product.reshape(SEQS, HEAD_DIM, COLUMNS) * ql_head[...][None]
        total[...] += jnp.sum(product, axis=1)

    expand(0, 0)

    @pl.loop(0, HEADS - 1)
    def _(head):
        slot = lax.rem(head, 2)
        expand(head + 1, 1 - slot)
        multiply(head, slot)

    multiply(HEADS - 1, (HEADS - 1) % 2)

    column = lax.broadcasted_iota(jnp.int32, (COLUMNS, QUERIES), 0)
    target = lax.broadcasted_iota(jnp.int32, (COLUMNS, QUERIES), 1)
    yq = g ^ (column // BLOCK)
    xq = (x - (column // 32) % N) & 3
    zq = (z - (column // 8) % N) & 3
    pick = ((g ^ zq) * 16 + xq * 4 + yq == target).astype(jnp.float32)
    picked = lax.dot_general(
        total[...], pick, (((1,), (0,)), ((), ())),
        preferred_element_type=jnp.float32, precision=lax.Precision.HIGHEST,
    )
    for m in range(N):
        out[m] = picked[:, 16 * m : 16 * (m + 1)]


def partial_scores(place, lefts, rights, eigen):
    return pl.pallas_call(
        score_kernel,
        out_shape=jax.ShapeDtypeStruct((N, SEQS, 16), jnp.float32),
        in_specs=[SMEM] + [VMEM] * 8 + [pl.BlockSpec(memory_space=pltpu.HBM)],
        out_specs=VMEM,
        scratch_shapes=[
            pltpu.VMEM((N, 2, HEADS, GRAD_RANK, HEAD_DIM), jnp.bfloat16),
            pltpu.VMEM((SEQS * GRAD_RANK, FEATURES), jnp.bfloat16),
            pltpu.VMEM((FEATURES, COLUMNS), jnp.bfloat16),
            pltpu.VMEM((HEAD_DIM, COLUMNS), jnp.float32),
            pltpu.VMEM((2, SEQS * HEAD_DIM, FEATURES), jnp.bfloat16),
            pltpu.VMEM((SEQS, COLUMNS), jnp.float32),
            pltpu.VMEM((HEADS, HEAD_DIM, FEATURES), jnp.bfloat16),
            pltpu.SemaphoreType.DMA((HEADS,)),
        ],
        compiler_params=pltpu.CompilerParams(vmem_limit_bytes=40 * 2**20),
    )(place, *lefts, *rights, pltpu.with_memory_space_constraint(eigen, pltpu.HBM))


def on_device(query_left, query_right, train_left, train_right, basis, eigen, counts):
    loop, g = lax.axis_index("loop"), lax.axis_index("head")
    place = jnp.stack([loop // 16, loop // 4 % 4, loop % 4, g]).astype(jnp.int32)

    left, right = rotated(query_left, query_right, train_left, basis)
    left = swapped(left, 0)

    both = jnp.concatenate([left[:1], right], 1)
    both = jnp.concatenate([both] + [along("z", both, s) for s in range(1, N)], 0)
    both = jnp.concatenate([both] + [along("x", both, s) for s in range(1, N)], 0)

    train_right = train_right.reshape(2, GRAD_RANK, TILES, 128).transpose(0, 2, 1, 3)
    rights = jnp.concatenate([both[:, HEADS:], train_right], 0)
    rights = [rights] + [along("y", rights, k) for k in range(1, N)]
    pair = jnp.concatenate([both[:, :HEADS], left[1:]], 0)
    pair = [pair, across_heads(pair, 2)]
    pair, rights = lax.optimization_barrier((pair, rights))
    lefts = [pair[0], across_heads(pair[0], 1), pair[1], across_heads(pair[1], 1)]
    partial = partial_scores(place, lefts, rights, eigen)

    summed = sum([across_heads(partial[m], m) for m in range(1, N)], partial[0])
    summed = sum([along("y", summed[2 * k : 2 * k + 2], -k) for k in range(1, N)], summed[:2])
    weights = counts.astype(jnp.float32) / 2048.0
    return (summed * weights[:, None] * FACTOR).T


def solution(mesh):
    placed = (
        P("loop", "head", None, None),
        P("loop", None, "head"),
        P("loop", "head", None, None),
        P("loop", None, "head"),
        P("head", None, None),
        P(None, None, "head"),
        P("loop"),
    )
    return jax.shard_map(
        on_device, mesh=mesh, in_specs=placed, out_specs=P("head", "loop"), check_vma=False
    )
```

```python
import functools
import math

import jax
import jax.numpy as jnp
from jax import lax
from jax.experimental import pallas as pl
from jax.experimental.pallas import tpu as pltpu
from jax.sharding import PartitionSpec as P

HEAD_COUNT = 32
HEAD_DIM = 128
MODEL_DIM = 4096
GRAD_RANK = 8
QUERIES = 64
DAMPING = 0.1
FACTOR = 1.0 / (GRAD_RANK * math.sqrt(HEAD_COUNT * HEAD_DIM * MODEL_DIM))

N = 4
HEADS = 8
SEQS = 8
FEATURES = 1024
COLUMNS = QUERIES * GRAD_RANK
BLOCK = COLUMNS // N


def axis_shift(axis, step):
    pairs = []
    for z in range(N):
        for x in range(N):
            for y in range(N):
                to = {"z": z, "x": x, "y": y}
                to[axis] = (to[axis] + step) % N
                pairs.append((z * 16 + x * 4 + y, to["z"] * 16 + to["x"] * 4 + to["y"]))
    return pairs


def swap_shift(step):
    pairs = []
    for z in range(N):
        for x in range(N):
            for y in range(N):
                for g in range(N):
                    source = (z * 16 + x * 4 + y) * N + g
                    target = (((z + step) % N) * 16 + x * 4 + g) * N + y
                    pairs.append((source, target))
    return pairs


def along(axis, value, step):
    return lax.ppermute(value, "loop", axis_shift(axis, step))


def swapped(value, step):
    return lax.ppermute(value, ("loop", "head"), swap_shift(step))


def across_heads(value, mask):
    return lax.ppermute(value, "head", [(i, i ^ mask) for i in range(N)])


VMEM = pl.BlockSpec(memory_space=pltpu.VMEM)
SMEM = pl.BlockSpec(memory_space=pltpu.SMEM)
TILES = FEATURES // 128


def rotate_kernel(query, right, train, train_right, basis, left_out, right_out, train_right_out):
    for h in range(HEADS):
        left = jnp.concatenate([query[0, h], train[0, h], train[1, h]], axis=0)
        left = jnp.dot(left, basis[h], preferred_element_type=jnp.float32).astype(jnp.bfloat16)
        for n in range(3):
            left_out[n, h] = left[8 * n : 8 * (n + 1)]
    for j in range(TILES):
        tile = slice(128 * j, 128 * (j + 1))
        right_out[0, j] = right[0, :, tile]
        train_right_out[0, j] = train_right[0, :, tile]
        train_right_out[1, j] = train_right[1, :, tile]


def rotated(query_left, query_right, train_left, train_right, basis):
    return pl.pallas_call(
        rotate_kernel,
        out_shape=(
            pltpu.VMEM((3, HEADS, GRAD_RANK, HEAD_DIM), jnp.bfloat16),
            pltpu.VMEM((1, TILES, GRAD_RANK, 128), jnp.bfloat16),
            pltpu.VMEM((2, TILES, GRAD_RANK, 128), jnp.bfloat16),
        ),
    )(query_left, query_right, train_left, train_right, basis)


def inverse_kernel(place, eigen, inverse, fetched, sems):
    fetches = [
        pltpu.make_async_copy(eigen.at[HEADS * place[2] + h], fetched.at[h], sems.at[h]) for h in range(HEADS)
    ]
    for fetch in fetches:
        fetch.start()
    for h, fetch in enumerate(fetches):
        fetch.wait()
        inverse[h] = 1.0 / (fetched[h].astype(jnp.float32) + DAMPING)


def inverses(place, eigen):
    return pl.pallas_call(
        inverse_kernel,
        out_shape=pltpu.VMEM((HEADS, HEAD_DIM, FEATURES), jnp.float32),
        in_specs=[SMEM, pl.BlockSpec(memory_space=pltpu.HBM)],
        out_specs=VMEM,
        scratch_shapes=[
            pltpu.VMEM((HEADS, HEAD_DIM, FEATURES), jnp.bfloat16),
            pltpu.SemaphoreType.DMA((HEADS,)),
        ],
        compiler_params=pltpu.CompilerParams(vmem_limit_bytes=16 * 2**20),
        cost_estimate=pl.CostEstimate(flops=2**21, bytes_accessed=6 * 2**20, transcendentals=2**20),
    )(place, pltpu.with_memory_space_constraint(eigen, pltpu.HBM))


def scale_kernel(place, *refs):
    tl = refs[0:4]
    tr = refs[4:8]
    inverse, scaled, tl_all, tr_all = refs[8:]
    y, g = place[2], place[3]
    for m in range(N):
        tl_all[lax.rem(y - (g ^ m) + N, N)] = tl[m][...]
    for k in range(N):
        for j in range(TILES):
            tr_all[16 * k : 16 * (k + 1), 128 * j : 128 * (j + 1)] = tr[k][:, j].reshape(16, 128)

    @pl.loop(0, HEADS)
    def _(head):
        left = tl_all[:, :, head].reshape(SEQS * GRAD_RANK, HEAD_DIM)
        left = jnp.concatenate([left] * SEQS, axis=1)
        own = lax.broadcasted_iota(jnp.int32, left.shape, 0) // GRAD_RANK
        own = own == lax.broadcasted_iota(jnp.int32, left.shape, 1) // HEAD_DIM
        left = jnp.where(own, left, jnp.zeros_like(left))
        dense = lax.dot_general(left, tr_all[...], (((0,), (0,)), ((), ())), preferred_element_type=jnp.float32)
        dense = dense.reshape(SEQS, HEAD_DIM, FEATURES) * inverse[head][None]
        scaled[head] = dense.astype(jnp.bfloat16).reshape(SEQS * HEAD_DIM, FEATURES)


def scaled_heads(place, tl, tr, inverse):
    return pl.pallas_call(
        scale_kernel,
        out_shape=pltpu.VMEM((HEADS, SEQS * HEAD_DIM, FEATURES), jnp.bfloat16),
        in_specs=[SMEM] + [VMEM] * 9,
        out_specs=VMEM,
        scratch_shapes=[
            pltpu.VMEM((N, 2, HEADS, GRAD_RANK, HEAD_DIM), jnp.bfloat16),
            pltpu.VMEM((SEQS * GRAD_RANK, FEATURES), jnp.bfloat16),
        ],
        compiler_params=pltpu.CompilerParams(vmem_limit_bytes=16 * 2**20),
        cost_estimate=pl.CostEstimate(flops=2**32, bytes_accessed=2**20, transcendentals=0),
    )(place, *tl, *tr, inverse)


def product_kernel(steps, last, place, *refs):
    ql = refs[0:4]
    qr = refs[4 : 4 + len(steps)]
    scaled, *rest = refs[4 + len(steps) :]
    if last:
        before, out, ql_all, qr_all, ql_head, total = rest
    else:
        total, ql_all, qr_all, ql_head = rest
    z, x, y, g = (place[i] for i in range(4))

    total[...] = jnp.zeros_like(total)
    for n, k in enumerate(steps):
        for j in range(TILES):
            block = qr[n][:, j].reshape(BLOCK, 128)
            qr_all[128 * j : 128 * (j + 1), BLOCK * n : BLOCK * (n + 1)] = block.T
        for m in range(N):

            @pl.when((g ^ ((y - k) & 3)) == m)
            def _(n=n, m=m):
                ql_all[n] = ql[m][...]

    @pl.loop(0, HEADS)
    def _(head):
        for n in range(len(steps)):
            block = ql_all[n, :, head].reshape(BLOCK, HEAD_DIM)
            ql_head[:, BLOCK * n : BLOCK * (n + 1)] = block.astype(jnp.float32).T
        product = jnp.dot(scaled[head], qr_all[...], preferred_element_type=jnp.float32)
        product = product.reshape(SEQS, HEAD_DIM, BLOCK * len(steps)) * ql_head[...][None]
        total[...] += jnp.sum(product, axis=1)

    if last:
        column = lax.broadcasted_iota(jnp.int32, (COLUMNS, QUERIES), 0)
        target = lax.broadcasted_iota(jnp.int32, (COLUMNS, QUERIES), 1)
        block = column // BLOCK
        yq = (y - 2 * block + (block // 2) * 3) & 3
        xq = (x - (column // 32) % N) & 3
        zq = (z - (column // 8) % N) & 3
        pick = ((g ^ zq) * 16 + xq * 4 + yq == target).astype(jnp.float32)
        both = jnp.concatenate([before[...], total[...]], axis=1)
        picked = lax.dot_general(
            both, pick, (((1,), (0,)), ((), ())),
            preferred_element_type=jnp.float32, precision=lax.Precision.HIGHEST,
        )
        for m in range(N):
            out[m] = picked[:, 16 * m : 16 * (m + 1)]


def products(place, steps, ql, qr, scaled, before=None):
    columns = BLOCK * len(steps)
    last = before is not None
    operands = [place, *ql, *qr, scaled] + ([before] if last else [])
    out = (N, SEQS, 16) if last else (SEQS, columns)
    scratch = [
        pltpu.VMEM((len(steps), 16, HEADS, GRAD_RANK, HEAD_DIM), jnp.bfloat16),
        pltpu.VMEM((FEATURES, columns), jnp.bfloat16),
        pltpu.VMEM((HEAD_DIM, columns), jnp.float32),
    ]
    return pl.pallas_call(
        functools.partial(product_kernel, steps, last),
        out_shape=jax.ShapeDtypeStruct(out, jnp.float32),
        in_specs=[SMEM] + [VMEM] * (len(operands) - 1),
        out_specs=VMEM,
        scratch_shapes=scratch + ([pltpu.VMEM((SEQS, columns), jnp.float32)] if last else []),
        compiler_params=pltpu.CompilerParams(vmem_limit_bytes=16 * 2**20),
        cost_estimate=pl.CostEstimate(flops=2**20, bytes_accessed=2**12, transcendentals=0),
    )(*operands)


def on_device(query_left, query_right, train_left, train_right, basis, eigen, counts):
    loop, g = lax.axis_index("loop"), lax.axis_index("head")
    place = jnp.stack([loop // 16, loop // 4 % 4, loop % 4, g]).astype(jnp.int32)

    left, right, train_right = rotated(query_left, query_right, train_left, train_right, basis)
    left = swapped(left, 0)

    both = jnp.concatenate([left[:1], right], 1)
    both = jnp.concatenate([both] + [along("z", both, s) for s in range(1, N)], 0)

    over_x = [along("x", both, s) for s in range(1, N)]
    tr = [train_right] + [along("y", train_right, k) for k in range(1, N)]
    pair = [left[1:], across_heads(left[1:], 2)]
    tl = [pair[0], across_heads(pair[0], 1), pair[1], across_heads(pair[1], 1)]
    inverse = inverses(place, eigen)
    both, over_x, tr, tl, inverse = lax.optimization_barrier((both, over_x, tr, tl, inverse))
    both = jnp.concatenate([both, *over_x], 0)

    scaled = scaled_heads(place, tl, tr, inverse)
    right = both[:, HEADS:]
    qr = [right] + [along("y", right, k) for k in range(1, N)]
    pair = [both[:, :HEADS], across_heads(both[:, :HEADS], 2)]
    pair, qr[2], scaled = lax.optimization_barrier((pair, qr[2], scaled))
    ql = [pair[0], across_heads(pair[0], 1), pair[1], across_heads(pair[1], 1)]
    first = products(place, (0, 2), ql, qr[0::2], scaled)
    partial = products(place, (1, 3), ql, qr[1::2], scaled, first)

    summed = sum([across_heads(partial[m], m) for m in range(1, N)], partial[0])
    summed = sum([along("y", summed[2 * k : 2 * k + 2], -k) for k in range(1, N)], summed[:2])
    weights = counts.astype(jnp.float32) / 2048.0
    return (summed * weights[:, None] * FACTOR).T


def solution(mesh):
    placed = (
        P("loop", "head", None, None),
        P("loop", None, "head"),
        P("loop", "head", None, None),
        P("loop", None, "head"),
        P("head", None, None),
        P(None, None, "head"),
        P("loop"),
    )
    return jax.shard_map(
        on_device, mesh=mesh, in_specs=placed, out_specs=P("head", "loop"), check_vma=False
    )
```

```python
import functools
import math

import jax
import jax.numpy as jnp
from jax import lax
from jax.experimental import pallas as pl
from jax.experimental.pallas import tpu as pltpu
from jax.sharding import PartitionSpec as P

HEAD_COUNT = 32
HEAD_DIM = 128
MODEL_DIM = 4096
GRAD_RANK = 8
QUERIES = 64
DAMPING = 0.1
FACTOR = 1.0 / (GRAD_RANK * math.sqrt(HEAD_COUNT * HEAD_DIM * MODEL_DIM))

N = 4
HEADS = 8
AT_ONCE = 4
SEQS = 8
FEATURES = 1024
COLUMNS = QUERIES * GRAD_RANK
BLOCK = COLUMNS // N


def axis_shift(axis, step):
    pairs = []
    for z in range(N):
        for x in range(N):
            for y in range(N):
                to = {"z": z, "x": x, "y": y}
                to[axis] = (to[axis] + step) % N
                pairs.append((z * 16 + x * 4 + y, to["z"] * 16 + to["x"] * 4 + to["y"]))
    return pairs


def swap_shift(step):
    pairs = []
    for z in range(N):
        for x in range(N):
            for y in range(N):
                for g in range(N):
                    source = (z * 16 + x * 4 + y) * N + g
                    target = (((z + step) % N) * 16 + x * 4 + g) * N + y
                    pairs.append((source, target))
    return pairs


def along(axis, value, step):
    return lax.ppermute(value, "loop", axis_shift(axis, step))


def swapped(value, step):
    return lax.ppermute(value, ("loop", "head"), swap_shift(step))


def across_heads(value, mask):
    return lax.ppermute(value, "head", [(i, i ^ mask) for i in range(N)])


VMEM = pl.BlockSpec(memory_space=pltpu.VMEM)
TILES = FEATURES // 128


def rotate_kernel(query, right, train, train_right, basis, left_out, right_out, train_right_out):
    for h in range(HEADS):
        left = jnp.concatenate([query[0, h], train[0, h], train[1, h]], axis=0)
        left = jnp.dot(left, basis[h], preferred_element_type=jnp.float32).astype(jnp.bfloat16)
        for n in range(3):
            left_out[n, h] = left[8 * n : 8 * (n + 1)]
    for j in range(TILES):
        tile = slice(128 * j, 128 * (j + 1))
        right_out[0, j] = right[0, :, tile]
        train_right_out[0, j] = train_right[0, :, tile]
        train_right_out[1, j] = train_right[1, :, tile]


def rotated(query_left, query_right, train_left, train_right, basis):
    return pl.pallas_call(
        rotate_kernel,
        out_shape=(
            pltpu.VMEM((3, HEADS, GRAD_RANK, HEAD_DIM), jnp.bfloat16),
            pltpu.VMEM((1, TILES, GRAD_RANK, 128), jnp.bfloat16),
            pltpu.VMEM((2, TILES, GRAD_RANK, 128), jnp.bfloat16),
        ),
    )(query_left, query_right, train_left, train_right, basis)


def place():
    loop = lax.axis_index("loop")
    return loop // 16, loop // 4 % 4, loop % 4, lax.axis_index("head")


def inverse_kernel(eigen, inverse, fetched, sems):
    _, _, y, _ = place()
    fetches = [pltpu.make_async_copy(eigen.at[HEADS * y + h], fetched.at[h], sems.at[h]) for h in range(HEADS)]
    for fetch in fetches:
        fetch.start()
    for h, fetch in enumerate(fetches):
        fetch.wait()
        inverse[h] = 1.0 / (fetched[h].astype(jnp.float32) + DAMPING)


def inverses(eigen):
    return pl.pallas_call(
        inverse_kernel,
        out_shape=pltpu.VMEM((HEADS, HEAD_DIM, FEATURES), jnp.float32),
        in_specs=[pl.BlockSpec(memory_space=pltpu.HBM)],
        out_specs=VMEM,
        scratch_shapes=[
            pltpu.VMEM((HEADS, HEAD_DIM, FEATURES), jnp.bfloat16),
            pltpu.SemaphoreType.DMA((HEADS,)),
        ],
        compiler_params=pltpu.CompilerParams(vmem_limit_bytes=16 * 2**20),
        cost_estimate=pl.CostEstimate(flops=2**21, bytes_accessed=6 * 2**20, transcendentals=2**20),
    )(pltpu.with_memory_space_constraint(eigen, pltpu.HBM))


def scale_kernel(*refs):
    tl = refs[0:4]
    tr = refs[4:8]
    inverse, scaled, tl_all, tr_all = refs[8:]
    _, _, y, g = place()
    for m in range(N):
        tl_all[lax.rem(y - (g ^ m) + N, N)] = tl[m][...]
    for k in range(N):
        for j in range(TILES):
            tr_all[16 * k : 16 * (k + 1), 128 * j : 128 * (j + 1)] = tr[k][:, j].reshape(16, 128)

    @pl.loop(0, HEADS, step=AT_ONCE)
    def _(head):
        lefts = []
        for h in range(AT_ONCE):
            left = tl_all[:, :, head + h].reshape(SEQS * GRAD_RANK, HEAD_DIM)
            left = jnp.concatenate([left] * SEQS, axis=1)
            own = lax.broadcasted_iota(jnp.int32, left.shape, 0) // GRAD_RANK
            own = own == lax.broadcasted_iota(jnp.int32, left.shape, 1) // HEAD_DIM
            lefts.append(jnp.where(own, left, jnp.zeros_like(left)))
        left = jnp.concatenate(lefts, axis=1)
        dense = lax.dot_general(left, tr_all[...], (((0,), (0,)), ((), ())), preferred_element_type=jnp.float32)
        dense = dense.reshape(AT_ONCE, SEQS, HEAD_DIM, FEATURES) * inverse[pl.ds(head, AT_ONCE)][:, None]
        scaled[pl.ds(head, AT_ONCE)] = dense.astype(jnp.bfloat16).reshape(AT_ONCE, SEQS * HEAD_DIM, FEATURES)


def scaled_heads(tl, tr, inverse):
    return pl.pallas_call(
        scale_kernel,
        out_shape=pltpu.VMEM((HEADS, SEQS * HEAD_DIM, FEATURES), jnp.bfloat16),
        in_specs=[VMEM] * 9,
        out_specs=VMEM,
        scratch_shapes=[
            pltpu.VMEM((N, 2, HEADS, GRAD_RANK, HEAD_DIM), jnp.bfloat16),
            pltpu.VMEM((SEQS * GRAD_RANK, FEATURES), jnp.bfloat16),
        ],
        compiler_params=pltpu.CompilerParams(vmem_limit_bytes=30 * 2**20),
        cost_estimate=pl.CostEstimate(flops=2**32, bytes_accessed=2**20, transcendentals=0),
    )(*tl, *tr, inverse)


def product_kernel(steps, last, *refs):
    ql = refs[0:4]
    qr = refs[4 : 4 + len(steps)]
    scaled, *rest = refs[4 + len(steps) :]
    if last:
        before, out, ql_all, qr_all, ql_head, total = rest
    else:
        total, ql_all, qr_all, ql_head = rest
    z, x, y, g = place()

    total[...] = jnp.zeros_like(total)
    for n, k in enumerate(steps):
        for j in range(TILES):
            block = qr[n][:, j].reshape(BLOCK, 128)
            qr_all[128 * j : 128 * (j + 1), BLOCK * n : BLOCK * (n + 1)] = block.T
        for m in range(N):

            @pl.when((g ^ ((y - k) & 3)) == m)
            def _(n=n, m=m):
                ql_all[n] = ql[m][...]

    @pl.loop(0, HEADS, step=AT_ONCE)
    def _(head):
        for h in range(AT_ONCE):
            for n in range(len(steps)):
                block = ql_all[n, :, head + h].reshape(BLOCK, HEAD_DIM)
                ql_head[h, :, BLOCK * n : BLOCK * (n + 1)] = block.astype(jnp.float32).T
        rows = scaled[pl.ds(head, AT_ONCE)].reshape(AT_ONCE * SEQS * HEAD_DIM, FEATURES)
        product = jnp.dot(rows, qr_all[...], preferred_element_type=jnp.float32)
        product = product.reshape(AT_ONCE, SEQS, HEAD_DIM, BLOCK * len(steps)) * ql_head[...][:, None]
        total[...] += jnp.sum(product, axis=(0, 2))

    if last:
        column = lax.broadcasted_iota(jnp.int32, (COLUMNS, QUERIES), 0)
        target = lax.broadcasted_iota(jnp.int32, (COLUMNS, QUERIES), 1)
        block = column // BLOCK
        yq = (y - 2 * block + (block // 2) * 3) & 3
        xq = (x - (column // 32) % N) & 3
        zq = (z - (column // 8) % N) & 3
        pick = ((g ^ zq) * 16 + xq * 4 + yq == target).astype(jnp.float32)
        both = jnp.concatenate([before[...], total[...]], axis=1)
        picked = lax.dot_general(
            both, pick, (((1,), (0,)), ((), ())),
            preferred_element_type=jnp.float32, precision=lax.Precision.HIGHEST,
        )
        for m in range(N):
            out[m] = picked[:, 16 * m : 16 * (m + 1)]


def products(steps, ql, qr, scaled, before=None):
    columns = BLOCK * len(steps)
    last = before is not None
    operands = [*ql, *qr, scaled] + ([before] if last else [])
    out = (N, SEQS, 16) if last else (SEQS, columns)
    scratch = [
        pltpu.VMEM((len(steps), 16, HEADS, GRAD_RANK, HEAD_DIM), jnp.bfloat16),
        pltpu.VMEM((FEATURES, columns), jnp.bfloat16),
        pltpu.VMEM((AT_ONCE, HEAD_DIM, columns), jnp.float32),
    ]
    return pl.pallas_call(
        functools.partial(product_kernel, steps, last),
        out_shape=jax.ShapeDtypeStruct(out, jnp.float32),
        in_specs=[VMEM] * len(operands),
        out_specs=VMEM,
        scratch_shapes=scratch + ([pltpu.VMEM((SEQS, columns), jnp.float32)] if last else []),
        compiler_params=pltpu.CompilerParams(vmem_limit_bytes=16 * 2**20),
        cost_estimate=pl.CostEstimate(flops=2**20, bytes_accessed=2**12, transcendentals=0),
    )(*operands)


def on_device(query_left, query_right, train_left, train_right, basis, eigen, counts):
    left, right, train_right = rotated(query_left, query_right, train_left, train_right, basis)
    left, train_right, inverse = lax.optimization_barrier((swapped(left, 0), train_right, inverses(eigen)))

    both = jnp.concatenate([left[:1], right], 1)
    over_z = [along("z", both, s) for s in range(1, N)]
    tr = [train_right] + [along("y", train_right, k) for k in range(1, N)]
    pair = [left[1:], across_heads(left[1:], 2)]
    over_z, tr[2], pair = lax.optimization_barrier((over_z, tr[2], pair))
    both = jnp.concatenate([both, *over_z], 0)

    over_x = [along("x", both, s) for s in range(1, N)]
    tl = [pair[0], across_heads(pair[0], 1), pair[1], across_heads(pair[1], 1)]
    over_x, tl, tr = lax.optimization_barrier((over_x, tl, tr))
    both = jnp.concatenate([both, *over_x], 0)

    scaled = scaled_heads(tl, tr, inverse)
    right = both[:, HEADS:]
    qr = [right] + [along("y", right, k) for k in range(1, N)]
    pair = [both[:, :HEADS], across_heads(both[:, :HEADS], 2)]
    pair, scaled = lax.optimization_barrier((pair, scaled))
    ql = [pair[0], across_heads(pair[0], 1), pair[1], across_heads(pair[1], 1)]
    first = products((0, 2), ql, qr[0::2], scaled)
    partial = products((1, 3), ql, qr[1::2], scaled, first)

    summed = sum([across_heads(partial[m], m) for m in range(1, N)], partial[0])
    summed = sum([along("y", summed[2 * k : 2 * k + 2], -k) for k in range(1, N)], summed[:2])
    weights = counts.astype(jnp.float32) / 2048.0
    return (summed * weights[:, None] * FACTOR).T


def solution(mesh):
    placed = (
        P("loop", "head", None, None),
        P("loop", None, "head"),
        P("loop", "head", None, None),
        P("loop", None, "head"),
        P("head", None, None),
        P(None, None, "head"),
        P("loop"),
    )
    return jax.shard_map(
        on_device, mesh=mesh, in_specs=placed, out_specs=P("head", "loop"), check_vma=False
    )
```

```python
import functools
import math

import jax
import jax.numpy as jnp
from jax import lax
from jax.experimental import pallas as pl
from jax.experimental.pallas import tpu as pltpu
from jax.sharding import PartitionSpec as P

HEAD_COUNT = 32
HEAD_DIM = 128
MODEL_DIM = 4096
GRAD_RANK = 8
QUERIES = 64
DAMPING = 0.1
FACTOR = 1.0 / (GRAD_RANK * math.sqrt(HEAD_COUNT * HEAD_DIM * MODEL_DIM))

N = 4
HEADS = 8
AT_ONCE = 4
SEQS = 8
FEATURES = 1024
COLUMNS = QUERIES * GRAD_RANK
BLOCK = COLUMNS // N


def axis_shift(axis, step):
    pairs = []
    for z in range(N):
        for x in range(N):
            for y in range(N):
                to = {"z": z, "x": x, "y": y}
                to[axis] = (to[axis] + step) % N
                pairs.append((z * 16 + x * 4 + y, to["z"] * 16 + to["x"] * 4 + to["y"]))
    return pairs


def swap_shift(step):
    pairs = []
    for z in range(N):
        for x in range(N):
            for y in range(N):
                for g in range(N):
                    source = (z * 16 + x * 4 + y) * N + g
                    target = (((z + step) % N) * 16 + x * 4 + g) * N + y
                    pairs.append((source, target))
    return pairs


def along(axis, value, step):
    return lax.ppermute(value, "loop", axis_shift(axis, step))


def swapped(value, step):
    return lax.ppermute(value, ("loop", "head"), swap_shift(step))


def across_heads(value, mask):
    return lax.ppermute(value, "head", [(i, i ^ mask) for i in range(N)])


VMEM = pl.BlockSpec(memory_space=pltpu.VMEM)
TILES = FEATURES // 128


def rotate_kernel(query, right, train, train_right, basis, left_out, right_out, train_right_out):
    for h in range(HEADS):
        left = jnp.concatenate([query[0, h], train[0, h], train[1, h]], axis=0)
        left = jnp.dot(left, basis[h], preferred_element_type=jnp.float32).astype(jnp.bfloat16)
        for n in range(3):
            left_out[n, h] = left[8 * n : 8 * (n + 1)]
    for j in range(TILES):
        tile = slice(128 * j, 128 * (j + 1))
        right_out[0, j] = right[0, :, tile]
        train_right_out[0, j] = train_right[0, :, tile]
        train_right_out[1, j] = train_right[1, :, tile]


def rotated(query_left, query_right, train_left, train_right, basis):
    return pl.pallas_call(
        rotate_kernel,
        out_shape=(
            pltpu.VMEM((3, HEADS, GRAD_RANK, HEAD_DIM), jnp.bfloat16),
            pltpu.VMEM((1, TILES, GRAD_RANK, 128), jnp.bfloat16),
            pltpu.VMEM((2, TILES, GRAD_RANK, 128), jnp.bfloat16),
        ),
    )(query_left, query_right, train_left, train_right, basis)


def place():
    loop = lax.axis_index("loop")
    return loop // 16, loop // 4 % 4, loop % 4, lax.axis_index("head")


def inverse_kernel(eigen, inverse, fetched, sems):
    _, _, y, _ = place()
    fetches = [pltpu.make_async_copy(eigen.at[HEADS * y + h], fetched.at[h], sems.at[h]) for h in range(HEADS)]
    for fetch in fetches:
        fetch.start()
    for h, fetch in enumerate(fetches):
        fetch.wait()
        inverse[h] = 1.0 / (fetched[h].astype(jnp.float32) + DAMPING)


def inverses(eigen):
    return pl.pallas_call(
        inverse_kernel,
        out_shape=pltpu.VMEM((HEADS, HEAD_DIM, FEATURES), jnp.float32),
        in_specs=[pl.BlockSpec(memory_space=pltpu.HBM)],
        out_specs=VMEM,
        scratch_shapes=[
            pltpu.VMEM((HEADS, HEAD_DIM, FEATURES), jnp.bfloat16),
            pltpu.SemaphoreType.DMA((HEADS,)),
        ],
        compiler_params=pltpu.CompilerParams(vmem_limit_bytes=16 * 2**20),
        cost_estimate=pl.CostEstimate(flops=2**21, bytes_accessed=6 * 2**20, transcendentals=2**20),
    )(pltpu.with_memory_space_constraint(eigen, pltpu.HBM))


def scale_kernel(*refs):
    tl = refs[0:4]
    tr = refs[4:8]
    inverse, scaled, tl_all, tr_all = refs[8:]
    _, _, y, g = place()
    for m in range(N):
        tl_all[lax.rem(y - (g ^ m) + N, N)] = tl[m][...]
    for k in range(N):
        for j in range(TILES):
            tr_all[16 * k : 16 * (k + 1), 128 * j : 128 * (j + 1)] = tr[k][:, j].reshape(16, 128)

    @pl.loop(0, HEADS, step=AT_ONCE)
    def _(head):
        lefts = []
        for h in range(AT_ONCE):
            left = tl_all[:, :, head + h].reshape(SEQS * GRAD_RANK, HEAD_DIM)
            left = jnp.concatenate([left] * SEQS, axis=1)
            own = lax.broadcasted_iota(jnp.int32, left.shape, 0) // GRAD_RANK
            own = own == lax.broadcasted_iota(jnp.int32, left.shape, 1) // HEAD_DIM
            lefts.append(jnp.where(own, left, jnp.zeros_like(left)))
        left = jnp.concatenate(lefts, axis=1)
        dense = lax.dot_general(left, tr_all[...], (((0,), (0,)), ((), ())), preferred_element_type=jnp.float32)
        dense = dense.reshape(AT_ONCE, SEQS, HEAD_DIM, FEATURES) * inverse[pl.ds(head, AT_ONCE)][:, None]
        scaled[pl.ds(head, AT_ONCE)] = dense.astype(jnp.bfloat16).reshape(AT_ONCE, SEQS * HEAD_DIM, FEATURES)


def scaled_heads(tl, tr, inverse):
    return pl.pallas_call(
        scale_kernel,
        out_shape=pltpu.VMEM((HEADS, SEQS * HEAD_DIM, FEATURES), jnp.bfloat16),
        in_specs=[VMEM] * 9,
        out_specs=VMEM,
        scratch_shapes=[
            pltpu.VMEM((N, 2, HEADS, GRAD_RANK, HEAD_DIM), jnp.bfloat16),
            pltpu.VMEM((SEQS * GRAD_RANK, FEATURES), jnp.bfloat16),
        ],
        compiler_params=pltpu.CompilerParams(vmem_limit_bytes=30 * 2**20),
        cost_estimate=pl.CostEstimate(flops=2**32, bytes_accessed=2**20, transcendentals=0),
    )(*tl, *tr, inverse)


def product_kernel(steps, last, *refs):
    ql = refs[0:4]
    qr = refs[4 : 4 + len(steps)]
    scaled, *rest = refs[4 + len(steps) :]
    if last:
        before, out, ql_all, qr_all, ql_head, total = rest
    else:
        total, ql_all, qr_all, ql_head = rest
    z, x, y, g = place()

    total[...] = jnp.zeros_like(total)
    for n, k in enumerate(steps):
        for j in range(TILES):
            block = qr[n][:, j].reshape(BLOCK, 128)
            qr_all[128 * j : 128 * (j + 1), BLOCK * n : BLOCK * (n + 1)] = block.T
        for m in range(N):

            @pl.when((g ^ ((y - k) & 3)) == m)
            def _(n=n, m=m):
                ql_all[n] = ql[m][...]

    @pl.loop(0, HEADS, step=AT_ONCE)
    def _(head):
        for h in range(AT_ONCE):
            for n in range(len(steps)):
                block = ql_all[n, :, head + h].reshape(BLOCK, HEAD_DIM)
                ql_head[h, :, BLOCK * n : BLOCK * (n + 1)] = block.astype(jnp.float32).T
        rows = scaled[pl.ds(head, AT_ONCE)].reshape(AT_ONCE * SEQS * HEAD_DIM, FEATURES)
        product = jnp.dot(rows, qr_all[...], preferred_element_type=jnp.float32)
        product = product.reshape(AT_ONCE, SEQS, HEAD_DIM, BLOCK * len(steps)) * ql_head[...][:, None]
        total[...] += jnp.sum(product, axis=(0, 2))

    if last:
        column = lax.broadcasted_iota(jnp.int32, (COLUMNS, QUERIES), 0)
        target = lax.broadcasted_iota(jnp.int32, (COLUMNS, QUERIES), 1)
        block = column // BLOCK
        yq = (y - 2 * block + (block // 2) * 3) & 3
        xq = (x - (column // 32) % N) & 3
        zq = (z - (column // 8) % N) & 3
        pick = ((g ^ zq) * 16 + xq * 4 + yq == target).astype(jnp.float32)
        both = jnp.concatenate([before[...], total[...]], axis=1)
        picked = lax.dot_general(
            both, pick, (((1,), (0,)), ((), ())),
            preferred_element_type=jnp.float32, precision=lax.Precision.HIGHEST,
        )
        for m in range(N):
            out[m] = picked[:, 16 * m : 16 * (m + 1)]


def products(steps, ql, qr, scaled, before=None):
    columns = BLOCK * len(steps)
    last = before is not None
    operands = [*ql, *qr, scaled] + ([before] if last else [])
    out = (N, SEQS, 16) if last else (SEQS, columns)
    scratch = [
        pltpu.VMEM((len(steps), 16, HEADS, GRAD_RANK, HEAD_DIM), jnp.bfloat16),
        pltpu.VMEM((FEATURES, columns), jnp.bfloat16),
        pltpu.VMEM((AT_ONCE, HEAD_DIM, columns), jnp.float32),
    ]
    return pl.pallas_call(
        functools.partial(product_kernel, steps, last),
        out_shape=jax.ShapeDtypeStruct(out, jnp.float32),
        in_specs=[VMEM] * len(operands),
        out_specs=VMEM,
        scratch_shapes=scratch + ([pltpu.VMEM((SEQS, columns), jnp.float32)] if last else []),
        compiler_params=pltpu.CompilerParams(vmem_limit_bytes=16 * 2**20),
        cost_estimate=pl.CostEstimate(flops=2**20, bytes_accessed=2**12, transcendentals=0),
    )(*operands)


def on_device(query_left, query_right, train_left, train_right, basis, eigen, counts):
    left, right, train_right = rotated(query_left, query_right, train_left, train_right, basis)
    left, train_right, inverse = lax.optimization_barrier((swapped(left, 0), train_right, inverses(eigen)))

    both = jnp.concatenate([left[:1], right], 1)
    over_z = [along("z", both, s) for s in range(1, N)]
    tr = [train_right] + [along("y", train_right, k) for k in range(1, N)]
    pair = [left[1:], across_heads(left[1:], 2)]
    over_z, tr[2], pair = lax.optimization_barrier((over_z, tr[2], pair))
    both = jnp.concatenate([both, *over_z], 0)

    over_x = [along("x", both, s) for s in range(1, N)]
    tl = [pair[0], across_heads(pair[0], 1), pair[1], across_heads(pair[1], 1)]
    over_x, tl, tr = lax.optimization_barrier((over_x, tl, tr))
    both = jnp.concatenate([both, *over_x], 0)

    scaled = scaled_heads(tl, tr, inverse)
    right = both[:, HEADS:]
    qr = [right] + [along("y", right, k) for k in range(1, N)]
    pair = [both[:, :HEADS], across_heads(both[:, :HEADS], 2)]
    ql = [pair[0], across_heads(pair[0], 1), pair[1], across_heads(pair[1], 1)]
    first = products((0, 2), ql, qr[0::2], scaled)
    partial = products((1, 3), ql, qr[1::2], scaled, first)

    summed = sum([across_heads(partial[m], m) for m in range(1, N)], partial[0])
    summed = sum([along("y", summed[2 * k : 2 * k + 2], -k) for k in range(1, N)], summed[:2])
    weights = counts.astype(jnp.float32) / 2048.0
    return (summed * weights[:, None] * FACTOR).T


def solution(mesh):
    placed = (
        P("loop", "head", None, None),
        P("loop", None, "head"),
        P("loop", "head", None, None),
        P("loop", None, "head"),
        P("head", None, None),
        P(None, None, "head"),
        P("loop"),
    )
    return jax.shard_map(
        on_device, mesh=mesh, in_specs=placed, out_specs=P("head", "loop"), check_vma=False
    )
```

```python
import functools
import math

import jax
import jax.numpy as jnp
from jax import lax
from jax.experimental import pallas as pl
from jax.experimental.pallas import tpu as pltpu
from jax.sharding import PartitionSpec as P

HEAD_COUNT = 32
HEAD_DIM = 128
MODEL_DIM = 4096
GRAD_RANK = 8
QUERIES = 64
DAMPING = 0.1
FACTOR = 1.0 / (GRAD_RANK * math.sqrt(HEAD_COUNT * HEAD_DIM * MODEL_DIM))

N = 4
HEADS = 8
AT_ONCE = 4
SEQS = 8
FEATURES = 1024
COLUMNS = QUERIES * GRAD_RANK
BLOCK = COLUMNS // N


def axis_shift(axis, step):
    pairs = []
    for z in range(N):
        for x in range(N):
            for y in range(N):
                to = {"z": z, "x": x, "y": y}
                to[axis] = (to[axis] + step) % N
                pairs.append((z * 16 + x * 4 + y, to["z"] * 16 + to["x"] * 4 + to["y"]))
    return pairs


def swap_shift(step):
    pairs = []
    for z in range(N):
        for x in range(N):
            for y in range(N):
                for g in range(N):
                    source = (z * 16 + x * 4 + y) * N + g
                    target = (((z + step) % N) * 16 + x * 4 + g) * N + y
                    pairs.append((source, target))
    return pairs


def along(axis, value, step):
    return lax.ppermute(value, "loop", axis_shift(axis, step))


def swapped(value, step):
    return lax.ppermute(value, ("loop", "head"), swap_shift(step))


def across_heads(value, mask):
    return lax.ppermute(value, "head", [(i, i ^ mask) for i in range(N)])


VMEM = pl.BlockSpec(memory_space=pltpu.VMEM)
TILES = FEATURES // 128


def rotate_kernel(query, right, train, train_right, basis, left_out, right_out, train_right_out):
    for h in range(HEADS):
        left = jnp.concatenate([query[0, h], train[0, h], train[1, h]], axis=0)
        left = jnp.dot(left, basis[h], preferred_element_type=jnp.float32).astype(jnp.bfloat16)
        for n in range(3):
            left_out[n, h] = left[8 * n : 8 * (n + 1)]
    for j in range(TILES):
        tile = slice(128 * j, 128 * (j + 1))
        right_out[0, j] = right[0, :, tile]
        train_right_out[0, j] = train_right[0, :, tile]
        train_right_out[1, j] = train_right[1, :, tile]


def rotated(query_left, query_right, train_left, train_right, basis):
    return pl.pallas_call(
        rotate_kernel,
        out_shape=(
            pltpu.VMEM((3, HEADS, GRAD_RANK, HEAD_DIM), jnp.bfloat16),
            pltpu.VMEM((1, TILES, GRAD_RANK, 128), jnp.bfloat16),
            pltpu.VMEM((2, TILES, GRAD_RANK, 128), jnp.bfloat16),
        ),
    )(query_left, query_right, train_left, train_right, basis)


def place():
    loop = lax.axis_index("loop")
    return loop // 16, loop // 4 % 4, loop % 4, lax.axis_index("head")


def inverse_kernel(eigen, inverse, fetched, sems):
    _, _, y, _ = place()
    fetches = [pltpu.make_async_copy(eigen.at[HEADS * y + h], fetched.at[h], sems.at[h]) for h in range(HEADS)]
    for fetch in fetches:
        fetch.start()
    for h, fetch in enumerate(fetches):
        fetch.wait()
        inverse[h] = 1.0 / (fetched[h].astype(jnp.float32) + DAMPING)


def inverses(eigen):
    return pl.pallas_call(
        inverse_kernel,
        out_shape=pltpu.VMEM((HEADS, HEAD_DIM, FEATURES), jnp.float32),
        in_specs=[pl.BlockSpec(memory_space=pltpu.HBM)],
        out_specs=VMEM,
        scratch_shapes=[
            pltpu.VMEM((HEADS, HEAD_DIM, FEATURES), jnp.bfloat16),
            pltpu.SemaphoreType.DMA((HEADS,)),
        ],
        compiler_params=pltpu.CompilerParams(vmem_limit_bytes=16 * 2**20),
        cost_estimate=pl.CostEstimate(flops=2**21, bytes_accessed=6 * 2**20, transcendentals=2**20),
    )(pltpu.with_memory_space_constraint(eigen, pltpu.HBM))


def scale_kernel(*refs):
    tl = refs[0:4]
    tr = refs[4:8]
    inverse, scaled, tl_all, tr_all = refs[8:]
    _, _, y, g = place()
    for m in range(N):
        tl_all[lax.rem(y - (g ^ m) + N, N)] = tl[m][...]
    for k in range(N):
        for j in range(TILES):
            tr_all[16 * k : 16 * (k + 1), 128 * j : 128 * (j + 1)] = tr[k][:, j].reshape(16, 128)

    @pl.loop(0, HEADS, step=AT_ONCE)
    def _(head):
        lefts = []
        for h in range(AT_ONCE):
            left = tl_all[:, :, head + h].reshape(SEQS * GRAD_RANK, HEAD_DIM)
            left = jnp.concatenate([left] * SEQS, axis=1)
            own = lax.broadcasted_iota(jnp.int32, left.shape, 0) // GRAD_RANK
            own = own == lax.broadcasted_iota(jnp.int32, left.shape, 1) // HEAD_DIM
            lefts.append(jnp.where(own, left, jnp.zeros_like(left)))
        left = jnp.concatenate(lefts, axis=1)
        dense = lax.dot_general(left, tr_all[...], (((0,), (0,)), ((), ())), preferred_element_type=jnp.float32)
        dense = dense.reshape(AT_ONCE, SEQS, HEAD_DIM, FEATURES) * inverse[pl.ds(head, AT_ONCE)][:, None]
        scaled[pl.ds(head, AT_ONCE)] = dense.astype(jnp.bfloat16).reshape(AT_ONCE, SEQS * HEAD_DIM, FEATURES)


def scaled_heads(tl, tr, inverse):
    return pl.pallas_call(
        scale_kernel,
        out_shape=pltpu.VMEM((HEADS, SEQS * HEAD_DIM, FEATURES), jnp.bfloat16),
        in_specs=[VMEM] * 9,
        out_specs=VMEM,
        scratch_shapes=[
            pltpu.VMEM((N, 2, HEADS, GRAD_RANK, HEAD_DIM), jnp.bfloat16),
            pltpu.VMEM((SEQS * GRAD_RANK, FEATURES), jnp.bfloat16),
        ],
        compiler_params=pltpu.CompilerParams(vmem_limit_bytes=30 * 2**20),
        cost_estimate=pl.CostEstimate(flops=2**32, bytes_accessed=2**20, transcendentals=0),
    )(*tl, *tr, inverse)


def product_kernel(steps, last, *refs):
    ql = refs[0:4]
    qr = refs[4 : 4 + len(steps)]
    scaled, *rest = refs[4 + len(steps) :]
    if last:
        before, out, ql_all, qr_all, ql_head, total = rest
    else:
        total, ql_all, qr_all, ql_head = rest
    z, x, y, g = place()

    total[...] = jnp.zeros_like(total)
    for n, k in enumerate(steps):
        for j in range(TILES):
            block = qr[n][:, j].reshape(BLOCK, 128)
            qr_all[128 * j : 128 * (j + 1), BLOCK * n : BLOCK * (n + 1)] = block.T
        for m in range(N):

            @pl.when((g ^ ((y - k) & 3)) == m)
            def _(n=n, m=m):
                ql_all[n] = ql[m][...]

    @pl.loop(0, HEADS, step=AT_ONCE)
    def _(head):
        for h in range(AT_ONCE):
            for n in range(len(steps)):
                block = ql_all[n, :, head + h].reshape(BLOCK, HEAD_DIM)
                ql_head[h, :, BLOCK * n : BLOCK * (n + 1)] = block.astype(jnp.float32).T
        rows = scaled[pl.ds(head, AT_ONCE)].reshape(AT_ONCE * SEQS * HEAD_DIM, FEATURES)
        product = jnp.dot(rows, qr_all[...], preferred_element_type=jnp.float32)
        product = product.reshape(AT_ONCE, SEQS, HEAD_DIM, BLOCK * len(steps)) * ql_head[...][:, None]
        total[...] += jnp.sum(product, axis=(0, 2))

    if last:
        column = lax.broadcasted_iota(jnp.int32, (COLUMNS, QUERIES), 0)
        target = lax.broadcasted_iota(jnp.int32, (COLUMNS, QUERIES), 1)
        block = column // BLOCK
        yq = (y - 2 * block + (block // 2) * 3) & 3
        xq = (x - (column // 32) % N) & 3
        zq = (z - (column // 8) % N) & 3
        pick = ((g ^ zq) * 16 + xq * 4 + yq == target).astype(jnp.float32)
        both = jnp.concatenate([before[...], total[...]], axis=1)
        high = both.astype(jnp.bfloat16).astype(jnp.float32)
        terms = jnp.concatenate([high, both - high], axis=0).astype(jnp.bfloat16)
        picked = jnp.dot(terms, pick.astype(jnp.bfloat16), preferred_element_type=jnp.float32)
        picked = picked[:SEQS] + picked[SEQS:]
        for m in range(N):
            out[m] = picked[:, 16 * m : 16 * (m + 1)]


def products(steps, ql, qr, scaled, before=None):
    columns = BLOCK * len(steps)
    last = before is not None
    operands = [*ql, *qr, scaled] + ([before] if last else [])
    out = (N, SEQS, 16) if last else (SEQS, columns)
    scratch = [
        pltpu.VMEM((len(steps), 16, HEADS, GRAD_RANK, HEAD_DIM), jnp.bfloat16),
        pltpu.VMEM((FEATURES, columns), jnp.bfloat16),
        pltpu.VMEM((AT_ONCE, HEAD_DIM, columns), jnp.float32),
    ]
    return pl.pallas_call(
        functools.partial(product_kernel, steps, last),
        out_shape=jax.ShapeDtypeStruct(out, jnp.float32),
        in_specs=[VMEM] * len(operands),
        out_specs=VMEM,
        scratch_shapes=scratch + ([pltpu.VMEM((SEQS, columns), jnp.float32)] if last else []),
        compiler_params=pltpu.CompilerParams(vmem_limit_bytes=16 * 2**20),
        cost_estimate=pl.CostEstimate(flops=2**20, bytes_accessed=2**12, transcendentals=0),
    )(*operands)


def on_device(query_left, query_right, train_left, train_right, basis, eigen, counts):
    left, right, train_right = rotated(query_left, query_right, train_left, train_right, basis)
    left, train_right, inverse = lax.optimization_barrier((swapped(left, 0), train_right, inverses(eigen)))

    both = jnp.concatenate([left[:1], right], 1)
    over_z = [along("z", both, s) for s in range(1, N)]
    tr = [train_right] + [along("y", train_right, k) for k in range(1, N)]
    pair = [left[1:], across_heads(left[1:], 2)]
    over_z, tr[2], pair = lax.optimization_barrier((over_z, tr[2], pair))
    both = jnp.concatenate([both, *over_z], 0)

    over_x = [along("x", both, s) for s in range(1, N)]
    tl = [pair[0], across_heads(pair[0], 1), pair[1], across_heads(pair[1], 1)]
    over_x, tl, tr = lax.optimization_barrier((over_x, tl, tr))
    both = jnp.concatenate([both, *over_x], 0)

    scaled = scaled_heads(tl, tr, inverse)
    right = both[:, HEADS:]
    qr = [right] + [along("y", right, k) for k in range(1, N)]
    pair = [both[:, :HEADS], across_heads(both[:, :HEADS], 2)]
    ql = [pair[0], across_heads(pair[0], 1), pair[1], across_heads(pair[1], 1)]
    first = products((0, 2), ql, qr[0::2], scaled)
    partial = products((1, 3), ql, qr[1::2], scaled, first)

    summed = sum([across_heads(partial[m], m) for m in range(1, N)], partial[0])
    summed = sum([along("y", summed[2 * k : 2 * k + 2], -k) for k in range(1, N)], summed[:2])
    weights = counts.astype(jnp.float32) / 2048.0
    return (summed * weights[:, None] * FACTOR).T


def solution(mesh):
    placed = (
        P("loop", "head", None, None),
        P("loop", None, "head"),
        P("loop", "head", None, None),
        P("loop", None, "head"),
        P("head", None, None),
        P(None, None, "head"),
        P("loop"),
    )
    return jax.shard_map(
        on_device, mesh=mesh, in_specs=placed, out_specs=P("head", "loop"), check_vma=False
    )
```
